256 devices in a mesh: space: 16 (over z, core), basis: 16 (over y, x).
Axes of the slice: x: 4, y: 4, z: 8, core: 2. Of those that a mesh axis runs over, the one named last changes fastest.
Arguments:
- basis_block: float32 [512, 196608], P('basis', 'space'), may hold values from -6 to 6
- schur: float32 [512, 512], P(('space', 'basis')), may hold values from -0.25 to 0.25
- kept: int32 [256], replicated, may hold values from 0 to 511, as said below
Outputs:
- rotated: float32 [256, 196608], P('basis', 'space')
The draws below stay inside these ranges and needn't reach their ends.
Inputs may be any that keep to these rules, and one draw needn't show every extreme that they name: `kept`: 256 different column indices; 0 and 511 are always among them.
All inputs are finite; a program needn't handle non-finite values.
Results may differ from the reference program's by a relative error of at most 0.00007.
Values sent between devices are 32-bit elements; how exact they have to be, the bound alone decides.
A program may use at most 128 MiB of HBM per device.

```python
import jax
import jax.numpy as jnp
from jax import lax

M = 512
K = 256
ROWS = 196608


def draw_kept(key, part):
    key = jax.random.fold_in(key, 7)
    first, second = jax.random.split(key)
    middle = jax.random.permutation(first, M - 2)[:K - 2].astype(jnp.int32) + 1
    ends = jnp.array([0, M - 1], jnp.int32)
    joined = jnp.concatenate([ends, middle])
    order = jax.random.permutation(second, K)
    return joined[order].astype(jnp.int32)


def shard_levels(own_key, dims, shards, low, top_value):
    factor_of, own = 1.0, jax.random.fold_in(own_key, 6)
    for axis_at, blocks in shards:
        steps = jnp.exp(jax.random.uniform(jax.random.fold_in(own, axis_at), (blocks,), jnp.float32, low / len(shards), top_value / len(shards)))
        factor_of = factor_of * jnp.repeat(steps, dims[axis_at] // blocks).reshape([-1 if axis == axis_at else 1 for axis in range(len(dims))])
    return factor_of


def gaussian(key, shape, spread, limit, pieces=(), kind=jnp.bfloat16):
    level = shard_levels(key, shape, pieces, -0.22, 0.18) if pieces else 1.0
    values = jax.random.normal(key, shape, jnp.float32) * spread * level
    return jnp.minimum(jnp.maximum(values, -limit), limit).astype(kind)


def setup_inputs(seed: int = 0) -> dict:
    seeds = jax.random.split(jax.random.key(seed), 4)
    basis_block = gaussian(seeds[0], (M, ROWS), 1.0, 6.0, ((0, 16), (1, 16)), jnp.float32)
    schur = gaussian(seeds[1], (M, M), M ** -0.5, 0.25, ((0, 256),), jnp.float32)
    kept = draw_kept(jax.random.fold_in(seeds[3], 71), 0)
    return dict(basis_block=basis_block, schur=schur, kept=kept)


def reference(basis_block, schur, kept):
    kept_block = schur[:, kept.astype(jnp.int32)]
    return jnp.dot(kept_block.T, basis_block, precision=lax.Precision.HIGHEST, preferred_element_type=jnp.float32)
```

```python
import jax
import jax.numpy as jnp
from jax import lax
from jax.sharding import PartitionSpec as P


def body(basis_block, schur, kept):
    selected = jnp.take(schur, kept, axis=1)
    kept_full = lax.all_gather(selected, ("space", "basis"), axis=0, tiled=True)
    columns = lax.all_to_all(basis_block, "basis", split_axis=1, concat_axis=0, tiled=True)
    product = jnp.dot(
        kept_full.T,
        columns,
        precision=lax.Precision.HIGHEST,
        preferred_element_type=jnp.float32,
    )
    return lax.all_to_all(product, "basis", split_axis=0, concat_axis=1, tiled=True)


def solution(mesh):
    in_specs = (P("basis", "space"), P(("space", "basis"), None), P())
    out_specs = P("basis", "space")
    return jax.shard_map(body, mesh=mesh, in_specs=in_specs, out_specs=out_specs, check_vma=False)
```

```python
import functools

import jax
import jax.numpy as jnp
from jax import lax
from jax.experimental import pallas as pl
from jax.experimental.pallas import tpu as pltpu
from jax.sharding import PartitionSpec as P

MESH = pl.DeviceIdType.MESH
NX, NY, NZ, NC = 4, 4, 8, 2
NB, NS = NX * NY, NZ * NC
CHUNKS = 3
PEERS = (
    (2, 2), (2, 1), (2, 3), (1, 2), (3, 2), (1, 1), (3, 3), (1, 3), (3, 1),
    (2, 0), (0, 2), (1, 0), (3, 0), (0, 1), (0, 3),
)
ZS = (1, 7, 2, 6, 3, 5, 4)


def kernel(basis, schur, kept, out, sel, k1, k2, kt, held, prod,
           b_send, b_recv, b_own, p_send, p_recv, p_own,
           s_send, s_recv, z_send, z_recv, f_send, f_recv):
    rows = basis.shape[0]
    own = out.shape[0]
    width = held.shape[3]
    block = CHUNKS * width
    space = lax.axis_index("space")
    me = lax.axis_index("basis")
    z, core = space // NC, lax.rem(space, NC)
    y, x = me // NX, lax.rem(me, NX)
    plane = [lax.rem(y + dy, NY) * NX + lax.rem(x + dx, NX) for dx, dy in PEERS]
    line = [lax.rem(z + d, NZ) for d in ZS]
    sibling = {"space": z * NC + 1 - core}

    barrier = pltpu.get_barrier_semaphore()
    for j in plane:
        pl.semaphore_signal(barrier, inc=1, device_id={"basis": j}, device_id_type=MESH)
    for zj in line:
        pl.semaphore_signal(barrier, inc=1, device_id={"space": zj * NC + core}, device_id_type=MESH)
    pl.semaphore_signal(barrier, inc=1, device_id=sibling, device_id_type=MESH)

    def columns(j, c):
        return pl.ds(pl.multiple_of(j * block + c * width, 128), width)

    for c in range(CHUNKS):
        pltpu.make_async_copy(basis.at[:, columns(me, c)], held.at[c, me], b_own.at[c]).start()

    index = lax.broadcasted_iota(jnp.int32, (schur.shape[1], kept.shape[1]), 0)
    one_hot = jnp.where(index == kept[...], 1.0, 0.0).astype(jnp.float32)
    sel[...] = jnp.dot(schur[...], one_hot, precision=lax.Precision.HIGHEST,
                       preferred_element_type=jnp.float32)

    pl.semaphore_wait(barrier, len(PEERS) + len(ZS) + 1)

    for j in plane:
        pltpu.make_async_remote_copy(
            src_ref=sel, dst_ref=k1.at[me], send_sem=s_send, recv_sem=s_recv,
            device_id={"basis": j}, device_id_type=MESH).start()

    def send_block(j, c):
        pltpu.make_async_remote_copy(
            src_ref=basis.at[:, columns(j, c)], dst_ref=held.at[c, me],
            send_sem=b_send.at[c], recv_sem=b_recv.at[c],
            device_id={"basis": j}, device_id_type=MESH).start()

    for j in plane:
        send_block(j, 0)

    k1[me] = sel[...]
    received = k1.at[pl.ds(0, NB - 1)]
    pltpu.make_async_copy(received, received, s_recv).wait()
    for j in range(NB):
        k2[z, core, 2 * j:2 * j + 2, :] = k1[j]
    mine = k2.at[z, core]
    for i, zj in enumerate(line):
        pltpu.make_async_remote_copy(
            src_ref=mine, dst_ref=mine, send_sem=z_send.at[i], recv_sem=z_recv.at[i],
            device_id={"space": zj * NC + core}, device_id_type=MESH).start()
    pltpu.make_async_remote_copy(
        src_ref=mine, dst_ref=mine, send_sem=f_send, recv_sem=f_recv,
        device_id=sibling, device_id_type=MESH).start()

    for c in range(1, CHUNKS):
        for j in plane:
            send_block(j, c)

    for i, d in enumerate(ZS):
        block_z = k2.at[lax.rem(z + NZ - d, NZ), core]
        pltpu.make_async_copy(block_z, block_z, z_recv.at[i]).wait()
        pltpu.make_async_remote_copy(
            src_ref=block_z, dst_ref=block_z, send_sem=f_send, recv_sem=f_recv,
            device_id=sibling, device_id_type=MESH).start()
    forwarded = k2.at[:, 0]
    pltpu.make_async_copy(forwarded, forwarded, f_recv).wait()
    kt[...] = k2[...].reshape(NS * rows, kept.shape[1]).T

    for c in range(CHUNKS):
        pltpu.make_async_copy(basis.at[:, columns(me, c)], held.at[c, me], b_own.at[c]).wait()
        others = held.at[c, pl.ds(0, NB - 1)]
        pltpu.make_async_copy(others, others, b_recv.at[c]).wait()
        result = jnp.dot(kt[...], held[c].reshape(NB * rows, width), precision=lax.Precision.HIGHEST,
                         preferred_element_type=jnp.float32)
        prod[c] = result.reshape(NB, own, width)
        for j in plane:
            pltpu.make_async_remote_copy(
                src_ref=prod.at[c, j], dst_ref=out.at[:, columns(me, c)],
                send_sem=p_send.at[c], recv_sem=p_recv.at[c],
                device_id={"basis": j}, device_id_type=MESH).start()
        pltpu.make_async_copy(prod.at[c, me], out.at[:, columns(me, c)], p_own.at[c]).start()

    pltpu.make_async_copy(received, received, s_send).wait()
    for i in range(len(ZS)):
        pltpu.make_async_copy(mine, mine, z_send.at[i]).wait()
    pltpu.make_async_copy(forwarded, forwarded, f_send).wait()
    for c in range(CHUNKS):
        others = held.at[c, pl.ds(0, NB - 1)]
        pltpu.make_async_copy(others, others, b_send.at[c]).wait()
        results = prod.at[c, pl.ds(0, NB - 1)]
        pltpu.make_async_copy(results, results, p_send.at[c]).wait()
        pltpu.make_async_copy(results, results, p_recv.at[c]).wait()
        pltpu.make_async_copy(prod.at[c, me], out.at[:, columns(me, c)], p_own.at[c]).wait()


def body(basis_block, schur, kept):
    rows, total = basis_block.shape
    picked = kept.shape[0]
    own = picked // NB
    width = total // NB // CHUNKS
    f32, vmem, dma = jnp.float32, pltpu.VMEM, pltpu.SemaphoreType.DMA
    return pl.pallas_call(
        kernel,
        out_shape=jax.ShapeDtypeStruct((own, total), f32),
        in_specs=[
            pl.BlockSpec(memory_space=pl.ANY),
            pl.BlockSpec(memory_space=vmem),
            pl.BlockSpec(memory_space=vmem),
        ],
        out_specs=pl.BlockSpec(memory_space=pl.ANY),
        scratch_shapes=[
            vmem((schur.shape[0], picked), f32),
            vmem((NB, schur.shape[0], picked), f32),
            vmem((NZ, NC, rows, picked), f32),
            vmem((picked, NB * rows), f32),
            vmem((CHUNKS, NB, rows, width), f32),
            vmem((CHUNKS, NB, own, width), f32),
            dma((CHUNKS,)), dma((CHUNKS,)), dma((CHUNKS,)),
            dma((CHUNKS,)), dma((CHUNKS,)), dma((CHUNKS,)),
            dma, dma, dma((len(ZS),)), dma((len(ZS),)), dma, dma,
        ],
        compiler_params=pltpu.CompilerParams(
            collective_id=0, has_side_effects=True, vmem_limit_bytes=40 << 20),
        cost_estimate=pl.CostEstimate(flops=2 * picked * NB * rows * width * CHUNKS, bytes_accessed=3 << 20, transcendentals=0),
    )(basis_block, schur, kept.reshape(1, picked))


def solution(mesh):
    in_specs = (P("basis", "space"), P(("space", "basis"), None), P())
    out_specs = P("basis", "space")
    return jax.shard_map(body, mesh=mesh, in_specs=in_specs, out_specs=out_specs, check_vma=False)
```

```python
import functools

import jax
import jax.numpy as jnp
from jax import lax
from jax.experimental import pallas as pl
from jax.experimental.pallas import tpu as pltpu
from jax.sharding import PartitionSpec as P

MESH = pl.DeviceIdType.MESH
NX, NY, NZ, NC = 4, 4, 8, 2
NB, NS = NX * NY, NZ * NC
CHUNKS = 3
PEERS = (
    (2, 2), (2, 1), (2, 3), (1, 2), (3, 2), (1, 1), (3, 3), (1, 3), (3, 1),
    (2, 0), (0, 2), (1, 0), (3, 0), (0, 1), (0, 3),
)
ZS = (1, 7, 2, 6, 3, 5, 4)


def kernel(basis, schur_in, kept_in, out, schur, kept, in_sem, sel, k1, k2, kt, held, prod,
           b_send, b_recv, b_own, p_send, p_recv, p_own,
           s_send, s_recv, z_send, z_recv, f_send, f_recv):
    rows = basis.shape[0]
    own = out.shape[0]
    width = held.shape[3]
    block = CHUNKS * width
    space = lax.axis_index("space")
    me = lax.axis_index("basis")
    z, core = space // NC, lax.rem(space, NC)
    y, x = me // NX, lax.rem(me, NX)
    plane = [lax.rem(y + dy, NY) * NX + lax.rem(x + dx, NX) for dx, dy in PEERS]
    line = [lax.rem(z + d, NZ) for d in ZS]
    sibling = {"space": z * NC + 1 - core}

    loads = [
        pltpu.make_async_copy(schur_in, schur, in_sem.at[0]),
        pltpu.make_async_copy(kept_in, kept, in_sem.at[1]),
    ]
    for load in loads:
        load.start()
    barrier = pltpu.get_barrier_semaphore()
    for j in plane:
        pl.semaphore_signal(barrier, inc=1, device_id={"basis": j}, device_id_type=MESH)
    for zj in line:
        pl.semaphore_signal(barrier, inc=1, device_id={"space": zj * NC + core}, device_id_type=MESH)
    pl.semaphore_signal(barrier, inc=1, device_id=sibling, device_id_type=MESH)

    def columns(j, c):
        return pl.ds(pl.multiple_of(j * block + c * width, 128), width)

    for c in range(CHUNKS):
        pltpu.make_async_copy(basis.at[:, columns(me, c)], held.at[c, me], b_own.at[c]).start()

    for load in loads:
        load.wait()
    index = lax.broadcasted_iota(jnp.int32, (schur.shape[1], kept.shape[1]), 0)
    one_hot = jnp.where(index == kept[...], 1.0, 0.0).astype(jnp.float32)
    sel[...] = jnp.dot(schur[...], one_hot, precision=lax.Precision.HIGHEST,
                       preferred_element_type=jnp.float32)

    pl.semaphore_wait(barrier, len(PEERS) + len(ZS) + 1)

    for j in plane:
        pltpu.make_async_remote_copy(
            src_ref=sel, dst_ref=k1.at[me], send_sem=s_send, recv_sem=s_recv,
            device_id={"basis": j}, device_id_type=MESH).start()

    def send_block(j, c):
        pltpu.make_async_remote_copy(
            src_ref=basis.at[:, columns(j, c)], dst_ref=held.at[c, me],
            send_sem=b_send.at[c], recv_sem=b_recv.at[c],
            device_id={"basis": j}, device_id_type=MESH).start()

    for j in plane:
        send_block(j, 0)

    k1[me] = sel[...]
    received = k1.at[pl.ds(0, NB - 1)]
    pltpu.make_async_copy(received, received, s_recv).wait()
    for j in range(NB):
        k2[z, core, 2 * j:2 * j + 2, :] = k1[j]
    mine = k2.at[z, core]
    for i, zj in enumerate(line):
        pltpu.make_async_remote_copy(
            src_ref=mine, dst_ref=mine, send_sem=z_send.at[i], recv_sem=z_recv.at[i],
            device_id={"space": zj * NC + core}, device_id_type=MESH).start()
    pltpu.make_async_remote_copy(
        src_ref=mine, dst_ref=mine, send_sem=f_send, recv_sem=f_recv,
        device_id=sibling, device_id_type=MESH).start()

    for c in range(1, CHUNKS):
        for j in plane:
            send_block(j, c)

    for i, d in enumerate(ZS):
        block_z = k2.at[lax.rem(z + NZ - d, NZ), core]
        pltpu.make_async_copy(block_z, block_z, z_recv.at[i]).wait()
        pltpu.make_async_remote_copy(
            src_ref=block_z, dst_ref=block_z, send_sem=f_send, recv_sem=f_recv,
            device_id=sibling, device_id_type=MESH).start()
    forwarded = k2.at[:, 0]
    pltpu.make_async_copy(forwarded, forwarded, f_recv).wait()
    kt[...] = k2[...].reshape(NS * rows, kept.shape[1]).T

    for c in range(CHUNKS):
        pltpu.make_async_copy(basis.at[:, columns(me, c)], held.at[c, me], b_own.at[c]).wait()
        others = held.at[c, pl.ds(0, NB - 1)]
        pltpu.make_async_copy(others, others, b_recv.at[c]).wait()
        result = jnp.dot(kt[...], held[c].reshape(NB * rows, width), precision=lax.Precision.HIGHEST,
                         preferred_element_type=jnp.float32)
        prod[c] = result.reshape(NB, own, width)
        for j in plane:
            pltpu.make_async_remote_copy(
                src_ref=prod.at[c, j], dst_ref=out.at[:, columns(me, c)],
                send_sem=p_send.at[c], recv_sem=p_recv.at[c],
                device_id={"basis": j}, device_id_type=MESH).start()
        pltpu.make_async_copy(prod.at[c, me], out.at[:, columns(me, c)], p_own.at[c]).start()

    pltpu.make_async_copy(received, received, s_send).wait()
    for i in range(len(ZS)):
        pltpu.make_async_copy(mine, mine, z_send.at[i]).wait()
    pltpu.make_async_copy(forwarded, forwarded, f_send).wait()
    for c in range(CHUNKS):
        others = held.at[c, pl.ds(0, NB - 1)]
        pltpu.make_async_copy(others, others, b_send.at[c]).wait()
        results = prod.at[c, pl.ds(0, NB - 1)]
        pltpu.make_async_copy(results, results, p_send.at[c]).wait()
        pltpu.make_async_copy(results, results, p_recv.at[c]).wait()
        pltpu.make_async_copy(prod.at[c, me], out.at[:, columns(me, c)], p_own.at[c]).wait()


def body(basis_block, schur, kept):
    rows, total = basis_block.shape
    picked = kept.shape[0]
    own = picked // NB
    width = total // NB // CHUNKS
    f32, vmem, dma = jnp.float32, pltpu.VMEM, pltpu.SemaphoreType.DMA
    return pl.pallas_call(
        kernel,
        out_shape=vmem((own, total), f32),
        in_specs=[
            pl.BlockSpec(memory_space=pltpu.HBM),
            pl.BlockSpec(memory_space=pltpu.HBM),
            pl.BlockSpec(memory_space=pltpu.HBM),
        ],
        out_specs=pl.BlockSpec(memory_space=pl.ANY),
        scratch_shapes=[
            vmem(schur.shape, f32),
            vmem((1, picked), jnp.int32),
            dma((2,)),
            vmem((schur.shape[0], picked), f32),
            vmem((NB, schur.shape[0], picked), f32),
            vmem((NZ, NC, rows, picked), f32),
            vmem((picked, NB * rows), f32),
            vmem((CHUNKS, NB, rows, width), f32),
            vmem((CHUNKS, NB, own, width), f32),
            dma((CHUNKS,)), dma((CHUNKS,)), dma((CHUNKS,)),
            dma((CHUNKS,)), dma((CHUNKS,)), dma((CHUNKS,)),
            dma, dma, dma((len(ZS),)), dma((len(ZS),)), dma, dma,
        ],
        compiler_params=pltpu.CompilerParams(
            collective_id=0, has_side_effects=True, vmem_limit_bytes=40 << 20),
        cost_estimate=pl.CostEstimate(flops=2 * picked * NB * rows * width * CHUNKS, bytes_accessed=3 << 20, transcendentals=0),
    )(*(pltpu.with_memory_space_constraint(a, pltpu.HBM) for a in (basis_block, schur, kept.reshape(1, picked))))


def solution(mesh):
    in_specs = (P("basis", "space"), P(("space", "basis"), None), P())
    out_specs = P("basis", "space")
    return jax.shard_map(body, mesh=mesh, in_specs=in_specs, out_specs=out_specs, check_vma=False)
```

```python
import functools

import jax
import jax.numpy as jnp
from jax import lax
from jax.experimental import pallas as pl
from jax.experimental.pallas import tpu as pltpu
from jax.sharding import PartitionSpec as P

MESH = pl.DeviceIdType.MESH
NX, NY, NZ, NC = 4, 4, 8, 2
NB, NS = NX * NY, NZ * NC
SHARES = (2, 2, 2)
LANE = 128
PEERS = (
    (2, 2), (2, 1), (2, 3), (1, 2), (3, 2), (1, 1), (3, 3), (1, 3), (3, 1),
    (2, 0), (0, 2), (1, 0), (3, 0), (0, 1), (0, 3),
)
FIRST = 15


def kernel(basis, schur_in, kept_in, out, schur, kept, in_sem, sel, k1, k2, kt,
           b_send, b_recv, b_own, p_send, p_recv, p_own,
           s_send, s_recv, z_send, z_recv, f_send, f_recv, higher, *chunks):
    count = len(SHARES)
    held, prod = chunks[:count], chunks[count:]
    rows = basis.shape[0]
    own = out.shape[0]
    block = LANE * sum(SHARES)
    space = lax.axis_index("space")
    me = lax.axis_index("basis")
    z, core = space // NC, lax.rem(space, NC)
    y, x = me // NX, lax.rem(me, NX)
    plane = [lax.rem(y + dy, NY) * NX + lax.rem(x + dx, NX) for dx, dy in PEERS]
    def at(level):
        return {"space": level * NC + core}

    sibling = {"space": z * NC + 1 - core}

    def tell(sem, device):
        pl.semaphore_signal(sem, inc=1, device_id=device, device_id_type=MESH)

    def copy_to(device, src, dst, send, recv):
        pltpu.make_async_remote_copy(
            src_ref=src, dst_ref=dst, send_sem=send, recv_sem=recv,
            device_id=device, device_id_type=MESH).start()

    def wait_for(ref, sem):
        pltpu.make_async_copy(ref, ref, sem).wait()

    def columns(j, c):
        first = j * block + LANE * sum(SHARES[:c])
        return pl.ds(pl.multiple_of(first, LANE), LANE * SHARES[c])

    barrier = pltpu.get_barrier_semaphore()
    for j in plane:
        tell(barrier, {"basis": j})
    for level in range(1, NZ):
        @pl.when(level > z)
        def _():
            tell(barrier, at(level))

    @pl.when(core == 1)
    def _():
        tell(barrier, sibling)

    loads = [
        pltpu.make_async_copy(schur_in, schur, in_sem.at[0]),
        pltpu.make_async_copy(kept_in, kept, in_sem.at[1]),
    ]
    for load in loads:
        load.start()
    for c in range(count):
        pltpu.make_async_copy(basis.at[:, columns(me, c)], held[c].at[me], b_own.at[c]).start()
    for load in loads:
        load.wait()
    index = lax.broadcasted_iota(jnp.int32, (schur.shape[1], kept.shape[1]), 0)
    one_hot = jnp.where(index == kept[...], 1.0, 0.0).astype(jnp.float32)
    sel[...] = jnp.dot(schur[...], one_hot, precision=lax.Precision.HIGHEST,
                       preferred_element_type=jnp.float32)

    pl.semaphore_wait(barrier, NB - 1 + z + 1 - core)
    for j in plane:
        copy_to({"basis": j}, sel, k1.at[me], s_send, s_recv)

    def send_blocks(first, last):
        for c, j in [(c, j) for c in range(count) for j in plane][first:last]:
            copy_to({"basis": j}, basis.at[:, columns(j, c)], held[c].at[me], b_send.at[c], b_recv.at[c])

    send_blocks(0, FIRST)

    for level in range(NZ - 1):
        @pl.when(level < z)
        def _():
            tell(higher, at(level))

    @pl.when(core == 0)
    def _():
        tell(higher, sibling)

    k1[me] = sel[...]
    received = k1.at[pl.ds(0, NB - 1)]
    wait_for(received, s_recv)
    for j in range(NB):
        k2[z, core, 2 * j:2 * j + 2, :] = k1[j]
    mine = k2.at[z, core]

    def send_level(level):
        d = lax.rem(level + NZ - z, NZ) - 1
        copy_to(at(level), mine, mine, z_send.at[d], z_recv.at[d])

    for level in range(NZ - 1):
        @pl.when(level < z)
        def _():
            send_level(level)

    send_blocks(FIRST, None)

    expected = NZ - 1 - z + core

    @pl.when(expected > 0)
    def _():
        pl.semaphore_wait(higher, expected)

    for level in range(1, NZ):
        @pl.when(level > z)
        def _():
            send_level(level)
    copy_to(sibling, mine, mine, f_send, f_recv)

    for level in range(NZ):
        @pl.when(level != z)
        def _():
            passed = k2.at[level, core]
            wait_for(passed, z_recv.at[lax.rem(z + NZ - level, NZ) - 1])
            copy_to(sibling, passed, passed, f_send, f_recv)
    forwarded = k2.at[:, 0]
    wait_for(forwarded, f_recv)
    kt[...] = k2[...].reshape(NS * rows, kept.shape[1]).T

    for c in range(count):
        pltpu.make_async_copy(basis.at[:, columns(me, c)], held[c].at[me], b_own.at[c]).wait()
        wait_for(held[c].at[pl.ds(0, NB - 1)], b_recv.at[c])
        result = jnp.dot(kt[...], held[c][...].reshape(NB * rows, -1), precision=lax.Precision.HIGHEST,
                         preferred_element_type=jnp.float32)
        prod[c][...] = result.reshape(NB, own, -1)
        for j in plane:
            copy_to({"basis": j}, prod[c].at[j], out.at[:, columns(me, c)], p_send.at[c], p_recv.at[c])
        pltpu.make_async_copy(prod[c].at[me], out.at[:, columns(me, c)], p_own.at[c]).start()

    wait_for(received, s_send)
    for d in range(NZ - 1):
        wait_for(mine, z_send.at[d])
    wait_for(forwarded, f_send)
    for c in range(count):
        wait_for(held[c].at[pl.ds(0, NB - 1)], b_send.at[c])
        results = prod[c].at[pl.ds(0, NB - 1)]
        wait_for(results, p_send.at[c])
        wait_for(results, p_recv.at[c])
        pltpu.make_async_copy(prod[c].at[me], out.at[:, columns(me, c)], p_own.at[c]).wait()


def body(basis_block, schur, kept):
    rows, total = basis_block.shape
    picked = kept.shape[0]
    own = picked // NB
    f32, vmem, dma = jnp.float32, pltpu.VMEM, pltpu.SemaphoreType.DMA
    regular = pltpu.SemaphoreType.REGULAR
    count = len(SHARES)
    operands = (basis_block, schur, kept.reshape(1, picked))
    return pl.pallas_call(
        kernel,
        out_shape=vmem((own, total), f32),
        in_specs=[pl.BlockSpec(memory_space=pltpu.HBM)] * 3,
        out_specs=pl.BlockSpec(memory_space=pl.ANY),
        scratch_shapes=[
            vmem(schur.shape, f32),
            vmem((1, picked), jnp.int32),
            dma((2,)),
            vmem((schur.shape[0], picked), f32),
            vmem((NB, schur.shape[0], picked), f32),
            vmem((NZ, NC, rows, picked), f32),
            vmem((picked, NB * rows), f32),
            dma((count,)), dma((count,)), dma((count,)),
            dma((count,)), dma((count,)), dma((count,)),
            dma, dma, dma((NZ - 1,)), dma((NZ - 1,)), dma, dma,
            regular,
            *(vmem((NB, rows, LANE * s), f32) for s in SHARES),
            *(vmem((NB, own, LANE * s), f32) for s in SHARES),
        ],
        compiler_params=pltpu.CompilerParams(
            collective_id=0, has_side_effects=True, vmem_limit_bytes=40 << 20),
        cost_estimate=pl.CostEstimate(flops=2 * picked * rows * total, bytes_accessed=3 << 20, transcendentals=0),
    )(*(pltpu.with_memory_space_constraint(a, pltpu.HBM) for a in operands))


def solution(mesh):
    in_specs = (P("basis", "space"), P(("space", "basis"), None), P())
    out_specs = P("basis", "space")
    return jax.shard_map(body, mesh=mesh, in_specs=in_specs, out_specs=out_specs, check_vma=False)
```

```python
import functools

import jax
import jax.numpy as jnp
from jax import lax
from jax.experimental import pallas as pl
from jax.experimental.pallas import tpu as pltpu
from jax.sharding import PartitionSpec as P

MESH = pl.DeviceIdType.MESH
NX, NY, NZ, NC = 4, 4, 8, 2
NB, NS = NX * NY, NZ * NC
SHARES = (1, 2, 1, 2)
LANE = 128
PEERS = (
    (2, 2), (2, 1), (2, 3), (1, 2), (3, 2), (1, 1), (3, 3), (1, 3), (3, 1),
    (2, 0), (0, 2), (1, 0), (3, 0), (0, 1), (0, 3),
)
FIRST = 30


def kernel(basis, schur_in, kept_in, out, schur, kept, in_sem, sel, k1, k2, kt,
           b_send, b_recv, b_own, p_send, p_recv, p_own,
           s_send, s_recv, z_send, z_recv, f_send, f_recv, higher, *chunks):
    count = len(SHARES)
    held, prod = chunks[:count], chunks[count:]
    rows = basis.shape[0]
    own = out.shape[0]
    block = LANE * sum(SHARES)
    space = lax.axis_index("space")
    me = lax.axis_index("basis")
    z, core = space // NC, lax.rem(space, NC)
    y, x = me // NX, lax.rem(me, NX)
    plane = [lax.rem(y + dy, NY) * NX + lax.rem(x + dx, NX) for dx, dy in PEERS]
    def at(level):
        return {"space": level * NC + core}

    sibling = {"space": z * NC + 1 - core}

    def tell(sem, device):
        pl.semaphore_signal(sem, inc=1, device_id=device, device_id_type=MESH)

    def copy_to(device, src, dst, send, recv):
        pltpu.make_async_remote_copy(
            src_ref=src, dst_ref=dst, send_sem=send, recv_sem=recv,
            device_id=device, device_id_type=MESH).start()

    def wait_for(ref, sem):
        pltpu.make_async_copy(ref, ref, sem).wait()

    def columns(j, c):
        first = j * block + LANE * sum(SHARES[:c])
        return pl.ds(pl.multiple_of(first, LANE), LANE * SHARES[c])

    barrier = pltpu.get_barrier_semaphore()
    for j in plane:
        tell(barrier, {"basis": j})
    for level in range(1, NZ):
        @pl.when(level > z)
        def _():
            tell(barrier, at(level))

    @pl.when(core == 1)
    def _():
        tell(barrier, sibling)

    loads = [
        pltpu.make_async_copy(schur_in, schur, in_sem.at[0]),
        pltpu.make_async_copy(kept_in, kept, in_sem.at[1]),
    ]
    for load in loads:
        load.start()
    for c in range(count):
        pltpu.make_async_copy(basis.at[:, columns(me, c)], held[c].at[me], b_own.at[c]).start()
    for load in loads:
        load.wait()
    index = lax.broadcasted_iota(jnp.int32, (schur.shape[1], kept.shape[1]), 0)
    one_hot = jnp.where(index == kept[...], 1.0, 0.0).astype(jnp.float32)
    sel[...] = jnp.dot(schur[...], one_hot, precision=lax.Precision.HIGHEST,
                       preferred_element_type=jnp.float32)

    pl.semaphore_wait(barrier, NB - 1 + z + 1 - core)
    for j in plane:
        copy_to({"basis": j}, sel, k1.at[me], s_send, s_recv)

    def send_blocks(first, last):
        for c, j in [(c, j) for c in range(count) for j in plane][first:last]:
            copy_to({"basis": j}, basis.at[:, columns(j, c)], held[c].at[me], b_send.at[c], b_recv.at[c])

    send_blocks(0, FIRST)

    for level in range(NZ - 1):
        @pl.when(level < z)
        def _():
            tell(higher, at(level))

    @pl.when(core == 0)
    def _():
        tell(higher, sibling)

    k1[me] = sel[...]
    received = k1.at[pl.ds(0, NB - 1)]
    wait_for(received, s_recv)
    for j in range(NB):
        k2[z, core, 2 * j:2 * j + 2, :] = k1[j]
    mine = k2.at[z, core]

    def send_level(level):
        d = lax.rem(level + NZ - z, NZ) - 1
        copy_to(at(level), mine, mine, z_send.at[d], z_recv.at[d])

    for level in range(NZ - 1):
        @pl.when(level < z)
        def _():
            send_level(level)

    send_blocks(FIRST, None)

    expected = NZ - 1 - z + core

    @pl.when(expected > 0)
    def _():
        pl.semaphore_wait(higher, expected)

    for level in range(1, NZ):
        @pl.when(level > z)
        def _():
            send_level(level)
    copy_to(sibling, mine, mine, f_send, f_recv)

    for level in range(NZ):
        @pl.when(level != z)
        def _():
            passed = k2.at[level, core]
            wait_for(passed, z_recv.at[lax.rem(z + NZ - level, NZ) - 1])
            copy_to(sibling, passed, passed, f_send, f_recv)
    forwarded = k2.at[:, 0]
    wait_for(forwarded, f_recv)
    kt[...] = k2[...].reshape(NS * rows, kept.shape[1]).T

    for c in range(count):
        pltpu.make_async_copy(basis.at[:, columns(me, c)], held[c].at[me], b_own.at[c]).wait()
        wait_for(held[c].at[pl.ds(0, NB - 1)], b_recv.at[c])
        result = jnp.dot(kt[...], held[c][...].reshape(NB * rows, -1), precision=lax.Precision.HIGHEST,
                         preferred_element_type=jnp.float32)
        prod[c][...] = result.reshape(NB, own, -1)
        for j in plane:
            copy_to({"basis": j}, prod[c].at[j], out.at[:, columns(me, c)], p_send.at[c], p_recv.at[c])
        pltpu.make_async_copy(prod[c].at[me], out.at[:, columns(me, c)], p_own.at[c]).start()

    wait_for(received, s_send)
    for d in range(NZ - 1):
        wait_for(mine, z_send.at[d])
    wait_for(forwarded, f_send)
    for c in range(count):
        wait_for(held[c].at[pl.ds(0, NB - 1)], b_send.at[c])
        results = prod[c].at[pl.ds(0, NB - 1)]
        wait_for(results, p_send.at[c])
        wait_for(results, p_recv.at[c])
        pltpu.make_async_copy(prod[c].at[me], out.at[:, columns(me, c)], p_own.at[c]).wait()


def body(basis_block, schur, kept):
    rows, total = basis_block.shape
    picked = kept.shape[0]
    own = picked // NB
    f32, vmem, dma = jnp.float32, pltpu.VMEM, pltpu.SemaphoreType.DMA
    regular = pltpu.SemaphoreType.REGULAR
    count = len(SHARES)
    operands = (basis_block, schur, kept.reshape(1, picked))
    return pl.pallas_call(
        kernel,
        out_shape=vmem((own, total), f32),
        in_specs=[pl.BlockSpec(memory_space=pltpu.HBM)] * 3,
        out_specs=pl.BlockSpec(memory_space=pl.ANY),
        scratch_shapes=[
            vmem(schur.shape, f32),
            vmem((1, picked), jnp.int32),
            dma((2,)),
            vmem((schur.shape[0], picked), f32),
            vmem((NB, schur.shape[0], picked), f32),
            vmem((NZ, NC, rows, picked), f32),
            vmem((picked, NB * rows), f32),
            dma((count,)), dma((count,)), dma((count,)),
            dma((count,)), dma((count,)), dma((count,)),
            dma, dma, dma((NZ - 1,)), dma((NZ - 1,)), dma, dma,
            regular,
            *(vmem((NB, rows, LANE * s), f32) for s in SHARES),
            *(vmem((NB, own, LANE * s), f32) for s in SHARES),
        ],
        compiler_params=pltpu.CompilerParams(
            collective_id=0, has_side_effects=True, vmem_limit_bytes=40 << 20),
        cost_estimate=pl.CostEstimate(flops=2 * picked * rows * total, bytes_accessed=3 << 20, transcendentals=0),
    )(*(pltpu.with_memory_space_constraint(a, pltpu.HBM) for a in operands))


def solution(mesh):
    in_specs = (P("basis", "space"), P(("space", "basis"), None), P())
    out_specs = P("basis", "space")
    return jax.shard_map(body, mesh=mesh, in_specs=in_specs, out_specs=out_specs, check_vma=False)
```

```python
import functools

import jax
import jax.numpy as jnp
from jax import lax
from jax.experimental import pallas as pl
from jax.experimental.pallas import tpu as pltpu
from jax.sharding import PartitionSpec as P

MESH = pl.DeviceIdType.MESH
NX, NY, NZ, NC = 4, 4, 8, 2
NB, NS = NX * NY, NZ * NC
SHARES = (1, 2, 1, 2)
LANE = 128
PEERS = (
    (2, 2), (2, 1), (2, 3), (1, 2), (3, 2), (1, 1), (3, 3), (1, 3), (3, 1),
    (2, 0), (0, 2), (1, 0), (3, 0), (0, 1), (0, 3),
)
FIRST = 22
SECOND = 30
AHEAD = 1


def kernel(basis, schur_in, kept_in, out, schur, kept, in_sem, sel, k1, k2, kt,
           b_send, b_recv, b_own, p_send, p_recv, p_own,
           s_send, s_recv, z_send, z_recv, f_send, f_recv, higher, *chunks):
    count = len(SHARES)
    held, prod = chunks[:count], chunks[count:]
    rows = basis.shape[0]
    own = out.shape[0]
    block = LANE * sum(SHARES)
    space = lax.axis_index("space")
    me = lax.axis_index("basis")
    z, core = space // NC, lax.rem(space, NC)
    y, x = me // NX, lax.rem(me, NX)
    plane = [lax.rem(y + dy, NY) * NX + lax.rem(x + dx, NX) for dx, dy in PEERS]
    def at(level):
        return {"space": level * NC + core}

    sibling = {"space": z * NC + 1 - core}

    def tell(sem, device):
        pl.semaphore_signal(sem, inc=1, device_id=device, device_id_type=MESH)

    def copy_to(device, src, dst, send, recv):
        pltpu.make_async_remote_copy(
            src_ref=src, dst_ref=dst, send_sem=send, recv_sem=recv,
            device_id=device, device_id_type=MESH).start()

    def wait_for(ref, sem):
        pltpu.make_async_copy(ref, ref, sem).wait()

    def columns(j, c):
        first = j * block + LANE * sum(SHARES[:c])
        return pl.ds(pl.multiple_of(first, LANE), LANE * SHARES[c])

    barrier = pltpu.get_barrier_semaphore()
    for j in plane:
        tell(barrier, {"basis": j})
    for level in range(1, NZ):
        @pl.when(level > z)
        def _():
            tell(barrier, at(level))

    @pl.when(core == 1)
    def _():
        tell(barrier, sibling)

    loads = [
        pltpu.make_async_copy(schur_in, schur, in_sem.at[0]),
        pltpu.make_async_copy(kept_in, kept, in_sem.at[1]),
    ]
    for load in loads:
        load.start()
    for c in range(count):
        pltpu.make_async_copy(basis.at[:, columns(me, c)], held[c].at[me], b_own.at[c]).start()
    for load in loads:
        load.wait()
    index = lax.broadcasted_iota(jnp.int32, (schur.shape[1], kept.shape[1]), 0)
    one_hot = jnp.where(index == kept[...], 1.0, 0.0).astype(jnp.float32)
    sel[...] = jnp.dot(schur[...], one_hot, precision=lax.Precision.HIGHEST,
                       preferred_element_type=jnp.float32)

    pl.semaphore_wait(barrier, NB - 1 + z + 1 - core)
    for j in plane:
        copy_to({"basis": j}, sel, k1.at[me], s_send, s_recv)

    def send_blocks(first, last):
        for c, j in [(c, j) for c in range(count) for j in plane][first:last]:
            copy_to({"basis": j}, basis.at[:, columns(j, c)], held[c].at[me], b_send.at[c], b_recv.at[c])

    send_blocks(0, FIRST)

    for level in range(NZ - 1):
        @pl.when(level < z)
        def _():
            tell(higher, at(level))

    @pl.when(core == 0)
    def _():
        tell(higher, sibling)

    k1[me] = sel[...]
    received = k1.at[pl.ds(0, NB - 1)]
    wait_for(received, s_recv)
    for j in range(NB):
        k2[z, core, 2 * j:2 * j + 2, :] = k1[j]
    mine = k2.at[z, core]

    def send_level(level):
        d = lax.rem(level + NZ - z, NZ) - 1
        copy_to(at(level), mine, mine, z_send.at[d], z_recv.at[d])

    for level in range(NZ - 1):
        @pl.when(level < z)
        def _():
            send_level(level)

    send_blocks(FIRST, SECOND)

    expected = NZ - 1 - z + core

    @pl.when(expected > 0)
    def _():
        pl.semaphore_wait(higher, expected)

    for level in range(1, NZ):
        @pl.when(level > z)
        def _():
            send_level(level)
    copy_to(sibling, mine, mine, f_send.at[0], f_recv.at[0])
    send_blocks(SECOND, None)


    levels = NZ // 2
    blocks = NB // 2
    quota = k2.at[pl.ds(0, levels), 0]

    def take_rows(part):
        half = lax.rem(z // levels + part, 2)
        for i in range(levels):
            level = half * levels + i

            @pl.when(level != z)
            def _():
                passed = k2.at[level, core]
                wait_for(passed, z_recv.at[lax.rem(z + NZ - level, NZ) - 1])
                copy_to(sibling, passed, passed, f_send.at[part], f_recv.at[part])

        wait_for(quota, f_recv.at[part])
        kt[part] = k2[pl.ds(half * levels, levels)].reshape(blocks * rows, kept.shape[1]).T

    def multiply(c, part):
        half = lax.rem(z // levels + part, 2)
        vectors = held[c][pl.ds(half * blocks, blocks)].reshape(blocks * rows, -1)
        result = jnp.dot(kt[part], vectors, precision=lax.Precision.HIGHEST, preferred_element_type=jnp.float32)
        return result.reshape(NB, own, -1)

    def take_chunk(c):
        pltpu.make_async_copy(basis.at[:, columns(me, c)], held[c].at[me], b_own.at[c]).wait()
        wait_for(held[c].at[pl.ds(0, NB - 1)], b_recv.at[c])

    def send_results(c):
        for j in plane:
            copy_to({"basis": j}, prod[c].at[j], out.at[:, columns(me, c)], p_send.at[c], p_recv.at[c])
        pltpu.make_async_copy(prod[c].at[me], out.at[:, columns(me, c)], p_own.at[c]).start()

    take_rows(0)
    for c in range(AHEAD):
        take_chunk(c)
        prod[c][...] = multiply(c, 0)
    take_rows(1)
    for c in range(AHEAD):
        prod[c][...] += multiply(c, 1)
        send_results(c)
    for c in range(AHEAD, count):
        take_chunk(c)
        prod[c][...] = multiply(c, 0) + multiply(c, 1)
        send_results(c)

    wait_for(received, s_send)
    for d in range(NZ - 1):
        wait_for(mine, z_send.at[d])
    for part in range(2):
        wait_for(quota, f_send.at[part])
    for c in range(count):
        wait_for(held[c].at[pl.ds(0, NB - 1)], b_send.at[c])
        results = prod[c].at[pl.ds(0, NB - 1)]
        wait_for(results, p_send.at[c])
        wait_for(results, p_recv.at[c])
        pltpu.make_async_copy(prod[c].at[me], out.at[:, columns(me, c)], p_own.at[c]).wait()


def body(basis_block, schur, kept):
    rows, total = basis_block.shape
    picked = kept.shape[0]
    own = picked // NB
    f32, vmem, dma = jnp.float32, pltpu.VMEM, pltpu.SemaphoreType.DMA
    regular = pltpu.SemaphoreType.REGULAR
    count = len(SHARES)
    operands = (basis_block, schur, kept.reshape(1, picked))
    return pl.pallas_call(
        kernel,
        out_shape=vmem((own, total), f32),
        in_specs=[pl.BlockSpec(memory_space=pltpu.HBM)] * 3,
        out_specs=pl.BlockSpec(memory_space=pl.ANY),
        scratch_shapes=[
            vmem(schur.shape, f32),
            vmem((1, picked), jnp.int32),
            dma((2,)),
            vmem((schur.shape[0], picked), f32),
            vmem((NB, schur.shape[0], picked), f32),
            vmem((NZ, NC, rows, picked), f32),
            vmem((2, picked, NB * rows // 2), f32),
            dma((count,)), dma((count,)), dma((count,)),
            dma((count,)), dma((count,)), dma((count,)),
            dma, dma, dma((NZ - 1,)), dma((NZ - 1,)), dma((2,)), dma((2,)),
            regular,
            *(vmem((NB, rows, LANE * s), f32) for s in SHARES),
            *(vmem((NB, own, LANE * s), f32) for s in SHARES),
        ],
        compiler_params=pltpu.CompilerParams(
            collective_id=0, has_side_effects=True, vmem_limit_bytes=40 << 20),
        cost_estimate=pl.CostEstimate(flops=2 * picked * rows * total, bytes_accessed=3 << 20, transcendentals=0),
    )(*(pltpu.with_memory_space_constraint(a, pltpu.HBM) for a in operands))


def solution(mesh):
    in_specs = (P("basis", "space"), P(("space", "basis"), None), P())
    out_specs = P("basis", "space")
    return jax.shard_map(body, mesh=mesh, in_specs=in_specs, out_specs=out_specs, check_vma=False)
```

```python
import functools

import jax
import jax.numpy as jnp
from jax import lax
from jax.experimental import pallas as pl
from jax.experimental.pallas import tpu as pltpu
from jax.sharding import PartitionSpec as P

MESH = pl.DeviceIdType.MESH
NX, NY, NZ, NC = 4, 4, 8, 2
NB, NS = NX * NY, NZ * NC
SHARES = (1, 2, 1, 2)
LANE = 128
PEERS = (
    (2, 2), (2, 1), (2, 3), (1, 2), (3, 2), (1, 1), (3, 3), (1, 3), (3, 1),
    (2, 0), (0, 2), (1, 0), (3, 0), (0, 1), (0, 3),
)
FIRST = 24
SECOND = 45
AHEAD = 1


def kernel(basis, schur_in, kept_in, out, schur, kept, in_sem, sel, k1, k2, kt,
           b_send, b_recv, b_own, p_send, p_recv, p_own,
           s_send, s_recv, z_send, z_recv, f_send, f_recv, higher, *chunks):
    count = len(SHARES)
    held, prod = chunks[:count], chunks[count:]
    rows = basis.shape[0]
    own = out.shape[0]
    block = LANE * sum(SHARES)
    space = lax.axis_index("space")
    me = lax.axis_index("basis")
    z, core = space // NC, lax.rem(space, NC)
    y, x = me // NX, lax.rem(me, NX)
    plane = [lax.rem(y + dy, NY) * NX + lax.rem(x + dx, NX) for dx, dy in PEERS]
    def at(level):
        return {"space": level * NC + core}

    sibling = {"space": z * NC + 1 - core}

    def tell(sem, device):
        pl.semaphore_signal(sem, inc=1, device_id=device, device_id_type=MESH)

    def copy_to(device, src, dst, send, recv):
        pltpu.make_async_remote_copy(
            src_ref=src, dst_ref=dst, send_sem=send, recv_sem=recv,
            device_id=device, device_id_type=MESH).start()

    def wait_for(ref, sem):
        pltpu.make_async_copy(ref, ref, sem).wait()

    def columns(j, c):
        first = j * block + LANE * sum(SHARES[:c])
        return pl.ds(pl.multiple_of(first, LANE), LANE * SHARES[c])

    barrier = pltpu.get_barrier_semaphore()
    for j in plane:
        tell(barrier, {"basis": j})
    for level in range(1, NZ):
        @pl.when(level > z)
        def _():
            tell(barrier, at(level))

    @pl.when(core == 1)
    def _():
        tell(barrier, sibling)

    loads = [
        pltpu.make_async_copy(schur_in, schur, in_sem.at[0]),
        pltpu.make_async_copy(kept_in, kept, in_sem.at[1]),
    ]
    for load in loads:
        load.start()
    for c in range(count):
        pltpu.make_async_copy(basis.at[:, columns(me, c)], held[c].at[me], b_own.at[c]).start()
    for load in loads:
        load.wait()
    index = lax.broadcasted_iota(jnp.int32, (schur.shape[1], kept.shape[1]), 0)
    one_hot = jnp.where(index == kept[...], 1.0, 0.0).astype(jnp.float32)
    sel[...] = jnp.dot(schur[...], one_hot, precision=lax.Precision.HIGHEST,
                       preferred_element_type=jnp.float32)

    pl.semaphore_wait(barrier, NB - 1 + z + 1 - core)

    for level in range(NZ - 1):
        @pl.when(level < z)
        def _():
            tell(higher, at(level))

    @pl.when(core == 0)
    def _():
        tell(higher, sibling)

    for j in plane:
        copy_to({"basis": j}, sel, k1.at[me], s_send, s_recv)

    def send_blocks(first, last):
        for c, j in [(c, j) for c in range(count) for j in plane][first:last]:
            copy_to({"basis": j}, basis.at[:, columns(j, c)], held[c].at[me], b_send.at[c], b_recv.at[c])

    send_blocks(0, FIRST)

    k1[me] = sel[...]
    received = k1.at[pl.ds(0, NB - 1)]
    wait_for(received, s_recv)
    for j in range(NB):
        k2[z, core, 2 * j:2 * j + 2, :] = k1[j]
    mine = k2.at[z, core]

    def send_level(level):
        d = lax.rem(level + NZ - z, NZ) - 1
        copy_to(at(level), mine, mine, z_send.at[d], z_recv.at[d])

    for level in range(NZ - 1):
        @pl.when(level < z)
        def _():
            send_level(level)

    send_blocks(FIRST, SECOND)

    expected = NZ - 1 - z + core

    @pl.when(expected > 0)
    def _():
        pl.semaphore_wait(higher, expected)

    for level in range(1, NZ):
        @pl.when(level > z)
        def _():
            send_level(level)
    copy_to(sibling, mine, mine, f_send.at[0], f_recv.at[0])
    send_blocks(SECOND, None)


    levels = NZ // 2
    blocks = NB // 2
    quota = k2.at[pl.ds(0, levels), 0]

    def take_rows(part):
        half = lax.rem(z // levels + part, 2)
        for i in range(levels):
            level = half * levels + i

            @pl.when(level != z)
            def _():
                passed = k2.at[level, core]
                wait_for(passed, z_recv.at[lax.rem(z + NZ - level, NZ) - 1])
                copy_to(sibling, passed, passed, f_send.at[part], f_recv.at[part])

        wait_for(quota, f_recv.at[part])
        kt[part] = k2[pl.ds(half * levels, levels)].reshape(blocks * rows, kept.shape[1]).T

    def multiply(c, part):
        half = lax.rem(z // levels + part, 2)
        vectors = held[c][pl.ds(half * blocks, blocks)].reshape(blocks * rows, -1)
        result = jnp.dot(kt[part], vectors, precision=lax.Precision.HIGHEST, preferred_element_type=jnp.float32)
        return result.reshape(NB, own, -1)

    def take_chunk(c):
        pltpu.make_async_copy(basis.at[:, columns(me, c)], held[c].at[me], b_own.at[c]).wait()
        wait_for(held[c].at[pl.ds(0, NB - 1)], b_recv.at[c])

    def send_results(c):
        for j in plane:
            copy_to({"basis": j}, prod[c].at[j], out.at[:, columns(me, c)], p_send.at[c], p_recv.at[c])
        pltpu.make_async_copy(prod[c].at[me], out.at[:, columns(me, c)], p_own.at[c]).start()

    take_rows(0)
    for c in range(AHEAD):
        take_chunk(c)
        prod[c][...] = multiply(c, 0)
    take_rows(1)
    for c in range(AHEAD):
        prod[c][...] += multiply(c, 1)
        send_results(c)
    for c in range(AHEAD, count):
        take_chunk(c)
        prod[c][...] = multiply(c, 0) + multiply(c, 1)
        send_results(c)

    wait_for(received, s_send)
    for d in range(NZ - 1):
        wait_for(mine, z_send.at[d])
    for part in range(2):
        wait_for(quota, f_send.at[part])
    for c in range(count):
        wait_for(held[c].at[pl.ds(0, NB - 1)], b_send.at[c])
        results = prod[c].at[pl.ds(0, NB - 1)]
        wait_for(results, p_send.at[c])
        wait_for(results, p_recv.at[c])
        pltpu.make_async_copy(prod[c].at[me], out.at[:, columns(me, c)], p_own.at[c]).wait()


def body(basis_block, schur, kept):
    rows, total = basis_block.shape
    picked = kept.shape[0]
    own = picked // NB
    f32, vmem, dma = jnp.float32, pltpu.VMEM, pltpu.SemaphoreType.DMA
    regular = pltpu.SemaphoreType.REGULAR
    count = len(SHARES)
    operands = (basis_block, schur, kept.reshape(1, picked))
    return pl.pallas_call(
        kernel,
        out_shape=vmem((own, total), f32),
        in_specs=[pl.BlockSpec(memory_space=pltpu.HBM)] * 3,
        out_specs=pl.BlockSpec(memory_space=pl.ANY),
        scratch_shapes=[
            vmem(schur.shape, f32),
            vmem((1, picked), jnp.int32),
            dma((2,)),
            vmem((schur.shape[0], picked), f32),
            vmem((NB, schur.shape[0], picked), f32),
            vmem((NZ, NC, rows, picked), f32),
            vmem((2, picked, NB * rows // 2), f32),
            dma((count,)), dma((count,)), dma((count,)),
            dma((count,)), dma((count,)), dma((count,)),
            dma, dma, dma((NZ - 1,)), dma((NZ - 1,)), dma((2,)), dma((2,)),
            regular,
            *(vmem((NB, rows, LANE * s), f32) for s in SHARES),
            *(vmem((NB, own, LANE * s), f32) for s in SHARES),
        ],
        compiler_params=pltpu.CompilerParams(
            collective_id=0, has_side_effects=True, vmem_limit_bytes=40 << 20),
        cost_estimate=pl.CostEstimate(flops=2 * picked * rows * total, bytes_accessed=3 << 20, transcendentals=0),
    )(*(pltpu.with_memory_space_constraint(a, pltpu.HBM) for a in operands))


def solution(mesh):
    in_specs = (P("basis", "space"), P(("space", "basis"), None), P())
    out_specs = P("basis", "space")
    return jax.shard_map(body, mesh=mesh, in_specs=in_specs, out_specs=out_specs, check_vma=False)
```

```python
import functools

import jax
import jax.numpy as jnp
from jax import lax
from jax.experimental import pallas as pl
from jax.experimental.pallas import tpu as pltpu
from jax.sharding import PartitionSpec as P

MESH = pl.DeviceIdType.MESH
NX, NY, NZ, NC = 4, 4, 8, 2
NB, NS = NX * NY, NZ * NC
SHARES = (1, 2, 1, 2)
LANE = 128
PEERS = (
    (2, 2), (2, 1), (2, 3), (1, 2), (3, 2), (1, 1), (3, 3), (1, 3), (3, 1),
    (2, 0), (0, 2), (1, 0), (3, 0), (0, 1), (0, 3),
)
FIRST = 22
SECOND = 30
AHEAD = 1


def kernel(basis, schur_in, kept_in, out, schur, kept, in_sem, sel, k1, k2, kt,
           b_send, b_recv, b_own, p_send, p_recv, p_own,
           s_send, s_recv, z_send, z_recv, f_send, f_recv, higher, *chunks):
    count = len(SHARES)
    held, prod = chunks[:count], chunks[count:]
    rows = basis.shape[0]
    own = out.shape[0]
    block = LANE * sum(SHARES)
    space = lax.axis_index("space")
    me = lax.axis_index("basis")
    z, core = space // NC, lax.rem(space, NC)
    y, x = me // NX, lax.rem(me, NX)
    turn = 1 - 2 * core
    plane = [lax.rem(y + turn * dy + NY, NY) * NX + lax.rem(x + turn * dx + NX, NX) for dx, dy in PEERS]
    def at(level):
        return {"space": level * NC + core}

    sibling = {"space": z * NC + 1 - core}

    def tell(sem, device):
        pl.semaphore_signal(sem, inc=1, device_id=device, device_id_type=MESH)

    def copy_to(device, src, dst, send, recv):
        pltpu.make_async_remote_copy(
            src_ref=src, dst_ref=dst, send_sem=send, recv_sem=recv,
            device_id=device, device_id_type=MESH).start()

    def wait_for(ref, sem):
        pltpu.make_async_copy(ref, ref, sem).wait()

    def columns(j, c):
        first = j * block + LANE * sum(SHARES[:c])
        return pl.ds(pl.multiple_of(first, LANE), LANE * SHARES[c])

    barrier = pltpu.get_barrier_semaphore()
    for j in plane:
        tell(barrier, {"basis": j})
    for level in range(1, NZ):
        @pl.when(level > z)
        def _():
            tell(barrier, at(level))

    @pl.when(core == 1)
    def _():
        tell(barrier, sibling)

    loads = [
        pltpu.make_async_copy(schur_in, schur, in_sem.at[0]),
        pltpu.make_async_copy(kept_in, kept, in_sem.at[1]),
    ]
    for load in loads:
        load.start()
    for c in range(count):
        pltpu.make_async_copy(basis.at[:, columns(me, c)], held[c].at[me], b_own.at[c]).start()
    for load in loads:
        load.wait()
    index = lax.broadcasted_iota(jnp.int32, (schur.shape[1], kept.shape[1]), 0)
    one_hot = jnp.where(index == kept[...], 1.0, 0.0).astype(jnp.float32)
    sel[...] = jnp.dot(schur[...], one_hot, precision=lax.Precision.HIGHEST,
                       preferred_element_type=jnp.float32)

    pl.semaphore_wait(barrier, NB - 1 + z + 1 - core)
    for j in plane:
        copy_to({"basis": j}, sel, k1.at[me], s_send, s_recv)

    def send_blocks(first, last):
        for c, j in [(c, j) for c in range(count) for j in plane][first:last]:
            copy_to({"basis": j}, basis.at[:, columns(j, c)], held[c].at[me], b_send.at[c], b_recv.at[c])

    send_blocks(0, FIRST)

    for level in range(NZ - 1):
        @pl.when(level < z)
        def _():
            tell(higher, at(level))

    @pl.when(core == 0)
    def _():
        tell(higher, sibling)

    k1[me] = sel[...]
    received = k1.at[pl.ds(0, NB - 1)]
    wait_for(received, s_recv)
    for j in range(NB):
        k2[z, core, 2 * j:2 * j + 2, :] = k1[j]
    mine = k2.at[z, core]

    def send_level(level):
        d = lax.rem(level + NZ - z, NZ) - 1
        copy_to(at(level), mine, mine, z_send.at[d], z_recv.at[d])

    for level in range(NZ - 1):
        @pl.when(level < z)
        def _():
            send_level(level)

    send_blocks(FIRST, SECOND)

    expected = NZ - 1 - z + core

    @pl.when(expected > 0)
    def _():
        pl.semaphore_wait(higher, expected)

    for level in range(1, NZ):
        @pl.when(level > z)
        def _():
            send_level(level)
    copy_to(sibling, mine, mine, f_send.at[0], f_recv.at[0])
    send_blocks(SECOND, None)


    levels = NZ // 2
    blocks = NB // 2
    quota = k2.at[pl.ds(0, levels), 0]

    def take_rows(part):
        half = lax.rem(z // levels + part, 2)
        for i in range(levels):
            level = half * levels + i

            @pl.when(level != z)
            def _():
                passed = k2.at[level, core]
                wait_for(passed, z_recv.at[lax.rem(z + NZ - level, NZ) - 1])
                copy_to(sibling, passed, passed, f_send.at[part], f_recv.at[part])

        wait_for(quota, f_recv.at[part])
        kt[part] = k2[pl.ds(half * levels, levels)].reshape(blocks * rows, kept.shape[1]).T

    def multiply(c, part):
        half = lax.rem(z // levels + part, 2)
        vectors = held[c][pl.ds(half * blocks, blocks)].reshape(blocks * rows, -1)
        result = jnp.dot(kt[part], vectors, precision=lax.Precision.HIGHEST, preferred_element_type=jnp.float32)
        return result.reshape(NB, own, -1)

    def take_chunk(c):
        pltpu.make_async_copy(basis.at[:, columns(me, c)], held[c].at[me], b_own.at[c]).wait()
        wait_for(held[c].at[pl.ds(0, NB - 1)], b_recv.at[c])

    def send_results(c):
        for j in plane:
            copy_to({"basis": j}, prod[c].at[j], out.at[:, columns(me, c)], p_send.at[c], p_recv.at[c])
        pltpu.make_async_copy(prod[c].at[me], out.at[:, columns(me, c)], p_own.at[c]).start()

    take_rows(0)
    for c in range(AHEAD):
        take_chunk(c)
        prod[c][...] = multiply(c, 0)
    take_rows(1)
    for c in range(AHEAD):
        prod[c][...] += multiply(c, 1)
        send_results(c)
    for c in range(AHEAD, count):
        take_chunk(c)
        prod[c][...] = multiply(c, 0) + multiply(c, 1)
        send_results(c)

    wait_for(received, s_send)
    for d in range(NZ - 1):
        wait_for(mine, z_send.at[d])
    for part in range(2):
        wait_for(quota, f_send.at[part])
    for c in range(count):
        wait_for(held[c].at[pl.ds(0, NB - 1)], b_send.at[c])
        results = prod[c].at[pl.ds(0, NB - 1)]
        wait_for(results, p_send.at[c])
        wait_for(results, p_recv.at[c])
        pltpu.make_async_copy(prod[c].at[me], out.at[:, columns(me, c)], p_own.at[c]).wait()


def body(basis_block, schur, kept):
    rows, total = basis_block.shape
    picked = kept.shape[0]
    own = picked // NB
    f32, vmem, dma = jnp.float32, pltpu.VMEM, pltpu.SemaphoreType.DMA
    regular = pltpu.SemaphoreType.REGULAR
    count = len(SHARES)
    operands = (basis_block, schur, kept.reshape(1, picked))
    return pl.pallas_call(
        kernel,
        out_shape=vmem((own, total), f32),
        in_specs=[pl.BlockSpec(memory_space=pltpu.HBM)] * 3,
        out_specs=pl.BlockSpec(memory_space=pl.ANY),
        scratch_shapes=[
            vmem(schur.shape, f32),
            vmem((1, picked), jnp.int32),
            dma((2,)),
            vmem((schur.shape[0], picked), f32),
            vmem((NB, schur.shape[0], picked), f32),
            vmem((NZ, NC, rows, picked), f32),
            vmem((2, picked, NB * rows // 2), f32),
            dma((count,)), dma((count,)), dma((count,)),
            dma((count,)), dma((count,)), dma((count,)),
            dma, dma, dma((NZ - 1,)), dma((NZ - 1,)), dma((2,)), dma((2,)),
            regular,
            *(vmem((NB, rows, LANE * s), f32) for s in SHARES),
            *(vmem((NB, own, LANE * s), f32) for s in SHARES),
        ],
        compiler_params=pltpu.CompilerParams(
            collective_id=0, has_side_effects=True, vmem_limit_bytes=40 << 20),
        cost_estimate=pl.CostEstimate(flops=2 * picked * rows * total, bytes_accessed=3 << 20, transcendentals=0),
    )(*(pltpu.with_memory_space_constraint(a, pltpu.HBM) for a in operands))


def solution(mesh):
    in_specs = (P("basis", "space"), P(("space", "basis"), None), P())
    out_specs = P("basis", "space")
    return jax.shard_map(body, mesh=mesh, in_specs=in_specs, out_specs=out_specs, check_vma=False)
```
